32 devices in a mesh: head: 4 (over y, core), blk: 8 (over z, x).
Axes of the slice: x: 2, y: 2, z: 4, core: 2. Of those that a mesh axis runs over, the one named last changes fastest.
Arguments:
- states: bfloat16 [8192, 4096], P('blk', 'head'), may hold values from -6 to 6
- qkv_weight: bfloat16 [3, 4096, 4096], P(None, None, 'head'), may hold values from -1 to 1
- norm_gains: bfloat16 [2, 4096], P(None, 'head'), may hold values from 0.5 to 2
- kv_cache: bfloat16 [2, 320, 64, 4096], P(None, 'blk', None, 'head'), may hold values from -300 to 300
- cached_len: int32 [8], replicated, may hold values from 1 to 2048, as said below
- old_table: int32 [8, 32], replicated, may hold values from -1 to 319, as said below
- new_table: int32 [8, 16], replicated, may hold values from 0 to 319, as said below
Outputs:
- attended: bfloat16 [8192, 4096], P('blk', 'head')
- updated_cache: bfloat16 [2, 320, 64, 4096], P(None, 'blk', None, 'head')
The draws below stay inside these ranges and needn't reach their ends.
Inputs may be any that keep to these rules, and one draw needn't show every extreme that they name: `cached_len`: one request has exactly 2048 cached tokens. old_table[r, b] is d * 40 plus a local slot for the blocks b of request r below the ceiling of cached_len[r] / 64, and -1 beyond; block b of request r lies on blk index d = (o + b) mod 8, where o is the index of its block 0. New block j of request r lies on blk index (p + j // 2) mod 8, where p is the index of its block 0; no slot appears twice in old_table and new_table together.
All inputs are finite; a program needn't handle non-finite values.
Results may differ from the reference program's by a relative error of at most 0.014.
The reference program's roundings to bfloat16 on the way count: a program that leaves them out, or rounds other values in their place, can miss the bound.
Values may be sent and summed in bfloat16 or wider, within the bound.
A program may use at most 192 MiB of HBM per device.

```python
import math
import jax
import jax.numpy as jnp
from jax import lax

D = 4096
HEADS = 32
HS = 128
TOK_DEV = 1024
REQS = 8
BT = 64
SLOTS = 40
LONG_DEV = 4
BLOCKS_DEV = 12
TOKENS = 8192
NEWR = 1024
GROUP = 1
MAXB = 32
NEWB = 16
POOL = 320
N_BLK = 8


def layout(key):
    base_key = jax.random.fold_in(key, 11)
    key_list = jax.random.split(base_key, 6)
    request_ids = jnp.arange(REQS, dtype=jnp.int32)
    longest = jax.random.randint(key_list[0], (), 0, REQS)
    shares = jax.random.randint(key_list[1], (REQS,), 4, 13)
    shares = jnp.where(request_ids == longest, 0, shares)
    spare_blocks = (BLOCKS_DEV - LONG_DEV) * N_BLK - (REQS - 1)
    portion = spare_blocks * shares // jnp.sum(shares)
    leftover = spare_blocks - jnp.sum(portion)
    receiver = jnp.where(longest == 0, 1, 0)
    portion = portion + jnp.where(request_ids == receiver, leftover, 0)
    block_count = jnp.where(request_ids == longest, MAXB, portion + 1)
    trims = jax.random.randint(key_list[2], (REQS,), 0, BT)
    trims = jnp.where(request_ids == longest, 0, trims)
    cached = block_count * BT - trims
    old_home = jax.random.randint(key_list[3], (REQS,), 0, N_BLK)
    new_home = jax.random.randint(key_list[4], (REQS,), 0, N_BLK)
    slot_scores = jax.random.randint(key_list[5], (N_BLK, SLOTS), 0, 1 << 20) * SLOTS + jnp.arange(SLOTS, dtype=jnp.int32)[None, :]
    slot_order = jnp.argsort(slot_scores, axis=1).astype(jnp.int32)
    devices = jnp.arange(N_BLK, dtype=jnp.int32)
    distance = (devices[None, :] - old_home[:, None]) % N_BLK
    old_counts = (block_count[:, None] - distance + N_BLK - 1) // N_BLK
    old_before = jnp.cumsum(old_counts, axis=0) - old_counts
    old_total = jnp.sum(old_counts, axis=0)
    new_distance = (devices[None, :] - new_home[:, None]) % N_BLK
    new_counts = jnp.where(new_distance < NEWB // 2, 2, 0)
    new_before = jnp.cumsum(new_counts, axis=0) - new_counts
    block_ids = jnp.arange(MAXB, dtype=jnp.int32)
    old_device = (old_home[:, None] + block_ids[None, :]) % N_BLK
    old_rank = old_before[request_ids[:, None], old_device] + block_ids[None, :] // N_BLK
    old_rank = jnp.clip(old_rank, 0, SLOTS - 1)
    old_slot = old_device * SLOTS + slot_order[old_device, old_rank]
    old_table = jnp.where(block_ids[None, :] < block_count[:, None], old_slot, -1).astype(jnp.int32)
    new_ids = jnp.arange(NEWB, dtype=jnp.int32)
    new_device = (new_home[:, None] + new_ids[None, :] // 2) % N_BLK
    new_rank = old_total[new_device] + new_before[request_ids[:, None], new_device] + new_ids[None, :] % 2
    new_table = (new_device * SLOTS + slot_order[new_device, new_rank]).astype(jnp.int32)
    return (cached.astype(jnp.int32), old_table, new_table)


def draw_cached_len(key, part):
    return layout(key)[0]


def draw_old_table(key, part):
    return layout(key)[1]


def draw_new_table(key, part):
    return layout(key)[2]


def draw_qkv_weight(key, part):
    columns = jnp.arange(D, dtype=jnp.int32) // HS
    level = columns.astype(jnp.float32) / (HEADS - 1)
    raw_values = jnp.clip(jax.random.normal(key, (3, D, D), jnp.float32), -6.0, 6.0)
    growth = 3.0 ** (0.5 * level)
    return (raw_values * growth[None, None, :] * D ** (-0.5)).astype(jnp.bfloat16)


def draw_kv_cache(key, part):
    return jnp.clip(jax.random.normal(key, (2, POOL, BT, D), jnp.float32), -6.0, 6.0).astype(jnp.bfloat16)


def steps_of(own_key, shape, pieces, least, largest):
    gain, own = 1.0, jax.random.fold_in(own_key, 6)
    for position, parts in pieces:
        heights = jnp.exp(jax.random.uniform(jax.random.fold_in(own, position), (parts,), jnp.float32, least / len(pieces), largest / len(pieces)))
        gain = gain * jnp.repeat(heights, shape[position] // parts).reshape([-1 if axis == position else 1 for axis in range(len(shape))])
    return gain


def normal_values(key, shape, width, reach, shards=(), kind=jnp.bfloat16):
    level = steps_of(key, shape, shards, -0.22, 0.18) if shards else 1.0
    drawn = jax.random.normal(key, shape, jnp.float32) * width * level
    return jnp.minimum(jnp.maximum(drawn, -reach), reach).astype(kind)


def setup_inputs(seed: int = 0) -> dict:
    streams_of = jax.random.split(jax.random.key(seed), 8)
    return {
        "states": normal_values(streams_of[0], (TOKENS, D), 1.0, 6.0, ((0, 8), (1, 4))),
        "qkv_weight": draw_qkv_weight(jax.random.fold_in(streams_of[7], 71), 0),
        "norm_gains": jnp.clip(jnp.exp(math.log(2.0) - 1.3862944 * jax.random.uniform(streams_of[2], (2, D), jnp.float32) ** steps_of(streams_of[2], (2, D), ((1, 4),), -0.2, 0.2)), 0.5, 2.0).astype(jnp.bfloat16),
        "kv_cache": draw_kv_cache(jax.random.fold_in(streams_of[7], 71), 0),
        "cached_len": draw_cached_len(jax.random.fold_in(streams_of[7], 71), 0),
        "old_table": draw_old_table(jax.random.fold_in(streams_of[7], 71), 0),
        "new_table": draw_new_table(jax.random.fold_in(streams_of[7], 71), 0),
    }


rope_base = 500000.0
norm_eps = 1e-06

def rotate(values, positions, head_size):
    half_size = head_size // 2
    frequency = rope_base ** (-jnp.arange(half_size, dtype=jnp.float32) * 2.0 / head_size)
    angles = positions.astype(jnp.float32)[:, None] * frequency[None, :]
    cosine = jnp.cos(angles)[:, None, :]
    sine_part = jnp.sin(angles)[:, None, :]
    first_half = values[..., :half_size]
    second = values[..., half_size:]
    return jnp.concatenate([first_half * cosine - second * sine_part, second * cosine + first_half * sine_part], axis=-1)

def reference(states, qkv_weight, norm_gains, kv_cache, cached_len, old_table, new_table):
    weight_full = qkv_weight.astype(jnp.float32)
    gains = norm_gains.astype(jnp.float32)
    outputs = []
    fresh_list = []
    score_scale = HS ** (-0.5)
    half_rows = TOK_DEV // 2
    for request in range(REQS):
        rows_raw = states[request * NEWR:(request + 1) * NEWR].astype(jnp.float32)
        split_rows = rows_raw.reshape(GROUP, 2, half_rows, D)
        rows_in = jnp.concatenate([split_rows[:, 0], split_rows[:, 1][::-1]], axis=0).reshape(NEWR, D)
        projected = jnp.einsum('tc,jcw->tjw', rows_in, weight_full)
        queries = projected[:, 0]
        key_new = projected[:, 1]
        value_new = projected[:, 2]
        queries = queries * lax.rsqrt(lax.optimization_barrier(jnp.mean(queries * queries, axis=1, keepdims=True)) + norm_eps) * gains[0]
        key_new = key_new * lax.rsqrt(lax.optimization_barrier(jnp.mean(key_new * key_new, axis=1, keepdims=True)) + norm_eps) * gains[1]
        positions = cached_len[request] + jnp.arange(NEWR, dtype=jnp.int32)
        queries = rotate(queries.reshape(NEWR, HEADS, HS), positions, HS).reshape(NEWR, D).astype(jnp.bfloat16)
        key_new = rotate(key_new.reshape(NEWR, HEADS, HS), positions, HS).reshape(NEWR, D).astype(jnp.bfloat16)
        value_new = value_new.astype(jnp.bfloat16)
        fresh_list.append(jnp.stack([key_new, value_new]))
        safe_slots = jnp.clip(old_table[request], 0, kv_cache.shape[1] - 1).astype(jnp.int32)
        cached = kv_cache[:, safe_slots].reshape(2, MAXB * BT, D)
        key_pos = jnp.arange(MAXB * BT, dtype=jnp.int32)
        cached_mask = jnp.broadcast_to(key_pos[None, :] < cached_len[request], (NEWR, MAXB * BT))
        token_ids = jnp.arange(NEWR, dtype=jnp.int32)
        causal = token_ids[None, :] <= token_ids[:, None]
        full_mask = jnp.concatenate([cached_mask, causal], axis=1)
        all_keys = jnp.concatenate([cached[0], key_new.astype(cached.dtype)], axis=0)
        all_values = jnp.concatenate([cached[1], value_new.astype(cached.dtype)], axis=0)

        def one_head(head_index):
            q_head = lax.dynamic_slice_in_dim(queries, head_index * HS, HS, 1).astype(jnp.float32)
            k_head = lax.dynamic_slice_in_dim(all_keys, head_index * HS, HS, 1).astype(jnp.float32)
            v_head = lax.dynamic_slice_in_dim(all_values, head_index * HS, HS, 1).astype(jnp.float32)
            scores = jnp.einsum('qd,kd->qk', q_head, k_head) * score_scale
            scores = jnp.where(full_mask, scores, -jnp.inf)
            row_max = lax.optimization_barrier(jnp.max(scores, axis=1, keepdims=True))
            weights = jnp.exp(scores - row_max)
            probabilities = (weights / lax.optimization_barrier(jnp.sum(weights, axis=1, keepdims=True))).astype(jnp.bfloat16)
            return jnp.dot(probabilities, v_head.astype(jnp.bfloat16), preferred_element_type=jnp.float32).astype(jnp.bfloat16)
        heads_out = lax.map(one_head, jnp.arange(HEADS, dtype=jnp.int32))
        token_major = jnp.transpose(heads_out, (1, 0, 2)).reshape(2 * GROUP, half_rows, D)
        back_rows = jnp.stack([token_major[:GROUP], token_major[GROUP:][::-1]], axis=1)
        outputs.append(back_rows.reshape(NEWR, D))
    attended = jnp.concatenate(outputs, axis=0)
    fresh_all = jnp.stack(fresh_list, axis=1).reshape(2, REQS * NEWB, BT, D).astype(kv_cache.dtype)
    updated_cache = kv_cache.at[:, new_table.reshape(-1).astype(jnp.int32)].set(fresh_all)
    return (attended, updated_cache)
```

```python
import functools

import jax
import jax.numpy as jnp
from jax import lax
from jax.experimental import pallas as pl
from jax.experimental.pallas import tpu as pltpu
from jax.sharding import PartitionSpec as P

D = 4096
HS = 128
PAIR = 2
NEAR = 2

rope_base = 500000.0
norm_eps = 1e-06
EXP2_SCALE = HS ** (-0.5) * 1.4426950408889634
LOW = -1e30
VMEM = 48 * 2**20


def swapped(block, axis, apart):
    count = lax.axis_size(axis)
    route = []
    for low in range(count):
        high = low | 1 << apart
        if high != low and high < count:
            route += [(low, high), (high, low)]
    return lax.ppermute(block, axis, route)


def pack_kernel(groups, group_size, slots, rounds, one, info, table, cache, near, far, sems):
    me = info[0]
    jobs = []
    for c in range(rounds):
        if c >= NEAR and one:
            jobs.append((c, info[1], far.at[c - NEAR]))
        else:
            for d in range(groups):
                ref = near.at[d, c] if c < NEAR else far.at[d, c - NEAR]
                jobs.append((c, d // group_size, ref))
    made = []
    for n, (c, r, ref) in enumerate(jobs):
        first = table[r, 0] // slots
        b = lax.rem(me - first + groups, groups) + groups * c
        entry = table[r, b]
        slot = jnp.clip(entry - me * slots, 0, slots - 1)
        copy = pltpu.make_async_copy(cache.at[:, slot], ref, sems.at[n])
        made.append((entry >= 0, copy))
        pl.when(entry >= 0)(copy.start)
    for there, copy in made:
        pl.when(there)(copy.wait)


def pack(kv_cache, info, old_table, groups, group_size, rounds, one):
    _, slots, length, width = kv_cache.shape
    near = (groups, NEAR, 2, length, width)
    far = (rounds - NEAR, 2, length, width)
    if not one:
        far = (groups,) + far
    hbm = pl.BlockSpec(memory_space=pl.ANY)
    return pl.pallas_call(
        functools.partial(pack_kernel, groups, group_size, slots, rounds, one),
        out_shape=[jax.ShapeDtypeStruct(near, jnp.bfloat16), jax.ShapeDtypeStruct(far, jnp.bfloat16)],
        grid_spec=pltpu.PrefetchScalarGridSpec(
            num_scalar_prefetch=2,
            grid=(1,),
            in_specs=[hbm],
            out_specs=[hbm, hbm],
            scratch_shapes=[pltpu.SemaphoreType.DMA((groups * rounds,))],
        ),
        name="pack",
    )(info, old_table, kv_cache)


def finish_kernel(heads, place, q_in, k_in, v_in, sums, gains, cosine, sine, q_out, k_out, sent):
    cos, sin = cosine[...], sine[...]
    scale = lax.rsqrt(sums[...] / D + norm_eps)
    for n, (raw, out) in enumerate(((q_in, q_out), (k_in, k_out))):
        for h in range(heads):
            cols = pl.ds(h * HS, HS)
            x = raw[:, cols] * scale[:, n : n + 1] * gains[n : n + 1, cols].astype(jnp.float32)
            y = (x * cos + pltpu.roll(x, HS // 2, 1) * sin).astype(jnp.bfloat16)
            out[:, cols] = y
            if n == 1:
                sent[0, 0, :, cols] = y
    sent[0, 1] = v_in[...]


def finish(place, q_raw, k_raw, v_new, sums, gains, cosine, sine, groups, tile):
    rows, width = q_raw.shape
    row = lambda w: pl.BlockSpec((tile, w), lambda t, place: (t, 0))
    return pl.pallas_call(
        functools.partial(finish_kernel, width // HS),
        out_shape=[
            jax.ShapeDtypeStruct((rows, width), jnp.bfloat16),
            jax.ShapeDtypeStruct((rows, width), jnp.bfloat16),
            jax.ShapeDtypeStruct((groups, 2, tile, width), jnp.bfloat16),
        ],
        grid_spec=pltpu.PrefetchScalarGridSpec(
            num_scalar_prefetch=1,
            grid=(rows // tile,),
            in_specs=[
                row(width), row(width), row(width), row(2),
                pl.BlockSpec((2, width), lambda t, place: (0, 0)),
                row(HS), row(HS),
            ],
            out_specs=[
                row(width), row(width),
                pl.BlockSpec((1, 2, tile, width), lambda t, place: (place[t], 0, 0, 0)),
            ],
        ),
        compiler_params=pltpu.CompilerParams(vmem_limit_bytes=VMEM),
        cost_estimate=pl.CostEstimate(flops=10 * rows * width, bytes_accessed=20 * rows * width, transcendentals=0),
        name="finish",
    )(place, q_raw, k_raw, v_new, sums, gains, cosine, sine)


def attend_kernel(groups, rounds, pieces, half, length, info, q_ref, k_ref, v_ref, near, far, out, acc, top, total):
    cached, first = info[0], info[1]
    span = groups * length

    def step(q, k, v, mask):
        s = lax.dot_general(q, k, (((1,), (1,)), ((), ())), preferred_element_type=jnp.float32)
        if mask is not None:
            s = jnp.where(mask, s, LOW)
        old = top[...]
        new = jnp.maximum(old, jnp.max(s, axis=1, keepdims=True))
        p = jnp.exp2((s - new[:, :1]) * EXP2_SCALE)
        shrink = jnp.exp2((old - new) * EXP2_SCALE)
        total[...] = total[...] * shrink + jnp.sum(p, axis=1, keepdims=True)
        acc[...] = acc[...] * shrink + jnp.dot(
            p.astype(jnp.bfloat16), v, preferred_element_type=jnp.float32
        )
        top[...] = new

    for part in range(2):
        mine = info[2 + part]
        rows = pl.ds(part * half, half)
        top[...] = jnp.full_like(top, LOW)
        total[...] = jnp.zeros_like(total)
        acc[...] = jnp.zeros_like(acc)
        for piece in range(pieces):
            theirs = info[4 + piece]
            keys = pl.ds(piece * half, half)

            @pl.when(theirs < mine)
            def _():
                step(q_ref[rows, :], k_ref[keys, :], v_ref[keys, :], None)

            @pl.when(theirs == mine)
            def _():
                a = lax.broadcasted_iota(jnp.int32, (half, half), 0)
                b = lax.broadcasted_iota(jnp.int32, (half, half), 1)
                step(q_ref[rows, :], k_ref[keys, :], v_ref[keys, :], b <= a)

        for c in range(rounds):
            ref, at = (near, c) if c < NEAR else (far, c - NEAR)

            @pl.when(cached >= (c + 1) * span)
            def _():
                k = ref[:, at, 0].reshape(span, HS)
                v = ref[:, at, 1].reshape(span, HS)
                step(q_ref[rows, :], k, v, None)

            @pl.when((cached > c * span) & (cached < (c + 1) * span))
            def _():
                k = ref[:, at, 0].reshape(span, HS)
                v = ref[:, at, 1].reshape(span, HS)

                def seen(shape, axis):
                    i = lax.broadcasted_iota(jnp.int32, shape, axis)
                    block = lax.rem(i // length - first + groups, groups) + groups * c
                    return block * length + lax.rem(i, length) < cached

                v = jnp.where(seen((span, HS), 0), v, jnp.zeros_like(v))
                step(q_ref[rows, :], k, v, seen((half, span), 1))

        out[rows, :] = (acc[...] / total[...]).astype(jnp.bfloat16)


def attend(info, queries, keys, values, near, far):
    rows, width = queries.shape
    groups, _, _, length, _ = near.shape
    rounds = near.shape[1] + far.shape[1]
    half = rows // 2
    pieces = keys.shape[0] // half
    flat = lambda n: pl.BlockSpec((n, HS), lambda h, info: (0, h))
    pool = lambda a: pl.BlockSpec(a.shape[:4] + (HS,), lambda h, info: (0, 0, 0, 0, h))
    count = keys.shape[0] + rounds * groups * length
    return pl.pallas_call(
        functools.partial(attend_kernel, groups, rounds, pieces, half, length),
        out_shape=jax.ShapeDtypeStruct((rows, width), jnp.bfloat16),
        grid_spec=pltpu.PrefetchScalarGridSpec(
            num_scalar_prefetch=1,
            grid=(width // HS,),
            in_specs=[flat(rows), flat(keys.shape[0]), flat(keys.shape[0]), pool(near), pool(far)],
            out_specs=flat(rows),
            scratch_shapes=[pltpu.VMEM((half, HS), jnp.float32)] * 3,
        ),
        compiler_params=pltpu.CompilerParams(vmem_limit_bytes=VMEM),
        cost_estimate=pl.CostEstimate(
            flops=8 * rows * width * count, bytes_accessed=4 * width * count, transcendentals=rows * count * width // HS
        ),
        name="attend",
    )(info, queries, keys, values, near, far)


def place_kernel(groups, group_size, half_pairs, slots, length, me_ref, table, arrived, cache, out, sems):
    me = me_ref[0]
    made = []
    for s in range(groups):
        r, m = s // group_size, s % group_size
        home = table[r, 0] // slots
        pair = lax.rem(me - home + groups, groups)
        here = (pair // half_pairs == m) | (pair // half_pairs == 2 * group_size - 1 - m)
        for i in range(PAIR):
            slot = jnp.clip(table[r, PAIR * pair + i] - me * slots, 0, slots - 1)
            copy = pltpu.make_async_copy(
                arrived.at[s, :, pl.ds(i * length, length)], out.at[:, slot], sems.at[s * PAIR + i]
            )
            made.append((here, copy))
            pl.when(here)(copy.start)
    for here, copy in made:
        pl.when(here)(copy.wait)


def place_new(me, new_table, arrived, kv_cache, groups, group_size, half_pairs):
    _, slots, length, _ = kv_cache.shape
    hbm = pl.BlockSpec(memory_space=pl.ANY)
    return pl.pallas_call(
        functools.partial(place_kernel, groups, group_size, half_pairs, slots, length),
        out_shape=jax.ShapeDtypeStruct(kv_cache.shape, kv_cache.dtype),
        grid_spec=pltpu.PrefetchScalarGridSpec(
            num_scalar_prefetch=2,
            grid=(1,),
            in_specs=[hbm, hbm],
            out_specs=hbm,
            scratch_shapes=[pltpu.SemaphoreType.DMA((groups * PAIR,))],
        ),
        input_output_aliases={3: 0},
        name="place",
    )(me, new_table, arrived, kv_cache)


def run(one, states, qkv_weight, norm_gains, kv_cache, cached_len, old_table, new_table):
    tok_rows = states.shape[0]
    half_rows = tok_rows // 2
    width = qkv_weight.shape[2]
    groups = lax.axis_size("blk")
    slots, length = kv_cache.shape[1:3]
    group_size = groups // cached_len.shape[0]
    rounds = old_table.shape[1] // groups
    me = lax.axis_index("blk").astype(jnp.int32)
    request, member = me // group_size, me % group_size
    late = 2 * group_size - 1 - member

    longest = jnp.argmax(old_table[:, NEAR * groups] >= 0).astype(jnp.int32)
    near, far = pack(kv_cache, jnp.stack([me, longest]), old_table, groups, group_size, rounds, one)
    near = lax.all_to_all(near, "blk", split_axis=0, concat_axis=0, tiled=True)
    if one:
        far = lax.all_gather(far, "blk", axis=0, tiled=False)
    else:
        far = lax.all_to_all(far, "blk", split_axis=0, concat_axis=0, tiled=True)

    whole = lax.all_gather(states, "head", axis=1, tiled=True)
    mul = lambda n: jnp.dot(whole, qkv_weight[n], preferred_element_type=jnp.float32)
    k_raw, q_raw = mul(1), mul(0)
    v_new = mul(2).astype(jnp.bfloat16)
    sums = lax.psum(
        jnp.stack([jnp.sum(q_raw * q_raw, axis=1), jnp.sum(k_raw * k_raw, axis=1)]), "head"
    ).T

    half_ids = jnp.arange(half_rows, dtype=jnp.int32)
    offset = jnp.concatenate([member * half_rows + half_ids, late * half_rows + half_ids])
    frequency = rope_base ** (-jnp.arange(HS // 2, dtype=jnp.float32) * 2.0 / HS)
    angles = (cached_len[request] + offset).astype(jnp.float32)[:, None] * frequency[None, :]
    cosine, sine = jnp.cos(angles), jnp.sin(angles)
    cosine = jnp.concatenate([cosine, cosine], axis=1)
    sine = jnp.concatenate([-sine, sine], axis=1)

    tile = PAIR * length
    half_pairs = half_rows // tile
    steps = jnp.arange(half_pairs, dtype=jnp.int32)
    pair = jnp.concatenate([member * half_pairs + steps, late * half_pairs + steps])
    place = (new_table[request, 0] // slots + pair) % groups
    queries, k_new, sent = finish(place, q_raw, k_raw, v_new, sums, norm_gains, cosine, sine, groups, tile)
    arrived = lax.all_to_all(sent, "blk", split_axis=0, concat_axis=0, tiled=True)

    keys, values = k_new, v_new
    for bit in range(group_size.bit_length() - 1):
        lower = member // 2**bit % 2 == 0
        both = []
        for mine in (keys, values):
            other = swapped(mine, "blk", bit)
            both.append(
                jnp.where(lower, jnp.concatenate([mine, other]), jnp.concatenate([other, mine]))
            )
        keys, values = both
    order = [p for m in range(group_size) for p in (m, 2 * group_size - 1 - m)]
    info = jnp.concatenate(
        [
            jnp.stack([cached_len[request], old_table[request, 0] // slots, member, late]),
            jnp.array(order, jnp.int32),
        ]
    ).astype(jnp.int32)
    attended = attend(info, queries, keys, values, near, far)
    updated = place_new(me[None], new_table, arrived, kv_cache, groups, group_size, half_pairs)
    return attended, updated


def body(*args):
    old_table = args[5]
    reach = NEAR * lax.axis_size("blk")
    alone = jnp.sum((old_table[:, reach] >= 0).astype(jnp.int32)) <= 1
    return lax.cond(alone, functools.partial(run, True), functools.partial(run, False), *args)


def solution(mesh):
    return jax.shard_map(
        body,
        mesh=mesh,
        in_specs=(
            P("blk", "head"),
            P(None, None, "head"),
            P(None, "head"),
            P(None, "blk", None, "head"),
            P(),
            P(),
            P(),
        ),
        out_specs=(P("blk", "head"), P(None, "blk", None, "head")),
        check_vma=False,
    )
```

```python
import functools

import jax
import jax.numpy as jnp
from jax import lax
from jax.experimental import pallas as pl
from jax.experimental.pallas import tpu as pltpu
from jax.sharding import PartitionSpec as P

D = 4096
HS = 128
PAIR = 2
NEAR = 2

rope_base = 500000.0
norm_eps = 1e-06
EXP2_SCALE = HS ** (-0.5) * 1.4426950408889634
LOW = -1e30
VMEM = 48 * 2**20


def swapped(block, axis, apart):
    count = lax.axis_size(axis)
    route = []
    for low in range(count):
        high = low | 1 << apart
        if high != low and high < count:
            route += [(low, high), (high, low)]
    return lax.ppermute(block, axis, route)


def move_kernel(info, table, block, *rest):
    rest[-1][...] = block[...].reshape(rest[-1].shape)


def pack_rounds(kv_cache, info, old_table, groups, group_size, start, stop, one):
    _, slots, length, width = kv_cache.shape
    count = stop - start
    places = 1 if one else groups

    def source(d, c, info, table):
        r = info[1] if one else d // group_size
        first = table[r, 0] // slots
        b = lax.rem(info[0] - first + groups, groups) + groups * (start + c)
        return 0, jnp.clip(table[r, b] - info[0] * slots, 0, slots - 1), 0, 0

    return pl.pallas_call(
        move_kernel,
        out_shape=jax.ShapeDtypeStruct((places, count, 2, length, width), jnp.bfloat16),
        grid_spec=pltpu.PrefetchScalarGridSpec(
            num_scalar_prefetch=2,
            grid=(places, count),
            in_specs=[pl.BlockSpec((2, 1, length, width), source)],
            out_specs=pl.BlockSpec((1, 1, 2, length, width), lambda d, c, info, table: (d, c, 0, 0, 0)),
        ),
        compiler_params=pltpu.CompilerParams(vmem_limit_bytes=VMEM),
        name="pack",
    )(info, old_table, kv_cache)


def pack(kv_cache, info, old_table, groups, group_size, rounds, one):
    near = pack_rounds(kv_cache, info, old_table, groups, group_size, 0, NEAR, False)
    far = pack_rounds(kv_cache, info, old_table, groups, group_size, NEAR, rounds, one)
    return near, far[0] if one else far


def finish_kernel(heads, place, q_in, k_in, v_in, sums, gains, cosine, sine, q_out, k_out, sent):
    cos, sin = cosine[...], sine[...]
    scale = lax.rsqrt(sums[...] / D + norm_eps)
    for n, (raw, out) in enumerate(((q_in, q_out), (k_in, k_out))):
        for h in range(heads):
            cols = pl.ds(h * HS, HS)
            x = raw[:, cols] * scale[:, n : n + 1] * gains[n : n + 1, cols].astype(jnp.float32)
            y = (x * cos + pltpu.roll(x, HS // 2, 1) * sin).astype(jnp.bfloat16)
            out[:, cols] = y
            if n == 1:
                sent[0, 0, :, cols] = y
    sent[0, 1] = v_in[...]


def finish(place, q_raw, k_raw, v_new, sums, gains, cosine, sine, groups, tile):
    rows, width = q_raw.shape
    row = lambda w: pl.BlockSpec((tile, w), lambda t, place: (t, 0))
    return pl.pallas_call(
        functools.partial(finish_kernel, width // HS),
        out_shape=[
            jax.ShapeDtypeStruct((rows, width), jnp.bfloat16),
            jax.ShapeDtypeStruct((rows, width), jnp.bfloat16),
            jax.ShapeDtypeStruct((groups, 2, tile, width), jnp.bfloat16),
        ],
        grid_spec=pltpu.PrefetchScalarGridSpec(
            num_scalar_prefetch=1,
            grid=(rows // tile,),
            in_specs=[
                row(width), row(width), row(width), row(2),
                pl.BlockSpec((2, width), lambda t, place: (0, 0)),
                row(HS), row(HS),
            ],
            out_specs=[
                row(width), row(width),
                pl.BlockSpec((1, 2, tile, width), lambda t, place: (place[t], 0, 0, 0)),
            ],
        ),
        compiler_params=pltpu.CompilerParams(vmem_limit_bytes=VMEM),
        cost_estimate=pl.CostEstimate(flops=10 * rows * width, bytes_accessed=20 * rows * width, transcendentals=0),
        name="finish",
    )(place, q_raw, k_raw, v_new, sums, gains, cosine, sine)


def attend_kernel(groups, rounds, pieces, half, length, info, q_ref, k_ref, v_ref, near, far, out, acc, top, total):
    cached, first = info[0], info[1]
    span = groups * length

    def step(q, k, v, mask):
        s = lax.dot_general(q, k, (((1,), (1,)), ((), ())), preferred_element_type=jnp.float32)
        if mask is not None:
            s = jnp.where(mask, s, LOW)
        old = top[...]
        new = jnp.maximum(old, jnp.max(s, axis=1, keepdims=True))
        p = jnp.exp2((s - new[:, :1]) * EXP2_SCALE)
        shrink = jnp.exp2((old - new) * EXP2_SCALE)
        total[...] = total[...] * shrink + jnp.sum(p, axis=1, keepdims=True)
        acc[...] = acc[...] * shrink + jnp.dot(
            p.astype(jnp.bfloat16), v, preferred_element_type=jnp.float32
        )
        top[...] = new

    for part in range(2):
        mine = info[2 + part]
        rows = pl.ds(part * half, half)
        top[...] = jnp.full_like(top, LOW)
        total[...] = jnp.zeros_like(total)
        acc[...] = jnp.zeros_like(acc)
        for piece in range(pieces):
            theirs = info[4 + piece]
            keys = pl.ds(piece * half, half)

            @pl.when(theirs < mine)
            def _():
                step(q_ref[rows, :], k_ref[keys, :], v_ref[keys, :], None)

            @pl.when(theirs == mine)
            def _():
                a = lax.broadcasted_iota(jnp.int32, (half, half), 0)
                b = lax.broadcasted_iota(jnp.int32, (half, half), 1)
                step(q_ref[rows, :], k_ref[keys, :], v_ref[keys, :], b <= a)

        for c in range(rounds):
            ref, at = (near, c) if c < NEAR else (far, c - NEAR)

            @pl.when(cached >= (c + 1) * span)
            def _():
                k = ref[:, at, 0].reshape(span, HS)
                v = ref[:, at, 1].reshape(span, HS)
                step(q_ref[rows, :], k, v, None)

            @pl.when((cached > c * span) & (cached < (c + 1) * span))
            def _():
                k = ref[:, at, 0].reshape(span, HS)
                v = ref[:, at, 1].reshape(span, HS)

                def seen(shape, axis):
                    i = lax.broadcasted_iota(jnp.int32, shape, axis)
                    block = lax.rem(i // length - first + groups, groups) + groups * c
                    return block * length + lax.rem(i, length) < cached

                v = jnp.where(seen((span, HS), 0), v, jnp.zeros_like(v))
                step(q_ref[rows, :], k, v, seen((half, span), 1))

        out[rows, :] = (acc[...] / total[...]).astype(jnp.bfloat16)


def attend(info, queries, keys, values, near, far):
    rows, width = queries.shape
    groups, _, _, length, _ = near.shape
    rounds = near.shape[1] + far.shape[1]
    half = rows // 2
    pieces = keys.shape[0] // half
    flat = lambda n: pl.BlockSpec((n, HS), lambda h, info: (0, h))
    pool = lambda a: pl.BlockSpec(a.shape[:4] + (HS,), lambda h, info: (0, 0, 0, 0, h))
    count = keys.shape[0] + rounds * groups * length
    return pl.pallas_call(
        functools.partial(attend_kernel, groups, rounds, pieces, half, length),
        out_shape=jax.ShapeDtypeStruct((rows, width), jnp.bfloat16),
        grid_spec=pltpu.PrefetchScalarGridSpec(
            num_scalar_prefetch=1,
            grid=(width // HS,),
            in_specs=[flat(rows), flat(keys.shape[0]), flat(keys.shape[0]), pool(near), pool(far)],
            out_specs=flat(rows),
            scratch_shapes=[pltpu.VMEM((half, HS), jnp.float32)] * 3,
        ),
        compiler_params=pltpu.CompilerParams(vmem_limit_bytes=VMEM),
        cost_estimate=pl.CostEstimate(
            flops=8 * rows * width * count, bytes_accessed=4 * width * count, transcendentals=rows * count * width // HS
        ),
        name="attend",
    )(info, queries, keys, values, near, far)


def place_new(me, new_table, arrived, kv_cache, groups, group_size, half_pairs):
    _, slots, length, width = kv_cache.shape
    requests = new_table.shape[0]

    def pair_of(r, me, table):
        return lax.rem(me[0] - table[r, 0] // slots + groups, groups)

    def source(r, i, me, table):
        part = pair_of(r, me, table) // half_pairs
        return r * group_size + jnp.minimum(part, 2 * group_size - 1 - part), 0, i, 0

    def target(r, i, me, table):
        slot = table[r, PAIR * pair_of(r, me, table) + i] - me[0] * slots
        return 0, jnp.clip(slot, 0, slots - 1), 0, 0

    return pl.pallas_call(
        move_kernel,
        out_shape=jax.ShapeDtypeStruct(kv_cache.shape, kv_cache.dtype),
        grid_spec=pltpu.PrefetchScalarGridSpec(
            num_scalar_prefetch=2,
            grid=(requests, PAIR),
            in_specs=[
                pl.BlockSpec((1, 2, length, width), source),
                pl.BlockSpec(memory_space=pl.ANY),
            ],
            out_specs=pl.BlockSpec((2, 1, length, width), target),
        ),
        input_output_aliases={3: 0},
        compiler_params=pltpu.CompilerParams(vmem_limit_bytes=VMEM),
        name="place",
    )(me, new_table, arrived, kv_cache)


def run(one, states, qkv_weight, norm_gains, kv_cache, cached_len, old_table, new_table):
    tok_rows = states.shape[0]
    half_rows = tok_rows // 2
    width = qkv_weight.shape[2]
    groups = lax.axis_size("blk")
    slots, length = kv_cache.shape[1:3]
    group_size = groups // cached_len.shape[0]
    rounds = old_table.shape[1] // groups
    me = lax.axis_index("blk").astype(jnp.int32)
    request, member = me // group_size, me % group_size
    late = 2 * group_size - 1 - member

    longest = jnp.argmax(old_table[:, NEAR * groups] >= 0).astype(jnp.int32)
    near, far = pack(kv_cache, jnp.stack([me, longest]), old_table, groups, group_size, rounds, one)
    near = lax.all_to_all(near, "blk", split_axis=0, concat_axis=0, tiled=True)
    if one:
        far = lax.all_gather(far, "blk", axis=0, tiled=False)
    else:
        far = lax.all_to_all(far, "blk", split_axis=0, concat_axis=0, tiled=True)

    whole = lax.all_gather(states, "head", axis=1, tiled=True)
    mul = lambda n: jnp.dot(whole, qkv_weight[n], preferred_element_type=jnp.float32)
    k_raw, q_raw = mul(1), mul(0)
    v_new = mul(2).astype(jnp.bfloat16)
    sums = lax.psum(
        jnp.stack([jnp.sum(q_raw * q_raw, axis=1), jnp.sum(k_raw * k_raw, axis=1)]), "head"
    ).T

    half_ids = jnp.arange(half_rows, dtype=jnp.int32)
    offset = jnp.concatenate([member * half_rows + half_ids, late * half_rows + half_ids])
    frequency = rope_base ** (-jnp.arange(HS // 2, dtype=jnp.float32) * 2.0 / HS)
    angles = (cached_len[request] + offset).astype(jnp.float32)[:, None] * frequency[None, :]
    cosine, sine = jnp.cos(angles), jnp.sin(angles)
    cosine = jnp.concatenate([cosine, cosine], axis=1)
    sine = jnp.concatenate([-sine, sine], axis=1)

    tile = PAIR * length
    half_pairs = half_rows // tile
    steps = jnp.arange(half_pairs, dtype=jnp.int32)
    pair = jnp.concatenate([member * half_pairs + steps, late * half_pairs + steps])
    place = (new_table[request, 0] // slots + pair) % groups
    queries, k_new, sent = finish(place, q_raw, k_raw, v_new, sums, norm_gains, cosine, sine, groups, tile)
    arrived = lax.all_to_all(sent, "blk", split_axis=0, concat_axis=0, tiled=True)

    keys, values = k_new, v_new
    for bit in range(group_size.bit_length() - 1):
        lower = member // 2**bit % 2 == 0
        both = []
        for mine in (keys, values):
            other = swapped(mine, "blk", bit)
            both.append(
                jnp.where(lower, jnp.concatenate([mine, other]), jnp.concatenate([other, mine]))
            )
        keys, values = both
    order = [p for m in range(group_size) for p in (m, 2 * group_size - 1 - m)]
    info = jnp.concatenate(
        [
            jnp.stack([cached_len[request], old_table[request, 0] // slots, member, late]),
            jnp.array(order, jnp.int32),
        ]
    ).astype(jnp.int32)
    attended = attend(info, queries, keys, values, near, far)
    updated = place_new(me[None], new_table, arrived, kv_cache, groups, group_size, half_pairs)
    return attended, updated


def body(*args):
    old_table = args[5]
    reach = NEAR * lax.axis_size("blk")
    alone = jnp.sum((old_table[:, reach] >= 0).astype(jnp.int32)) <= 1
    return lax.cond(alone, functools.partial(run, True), functools.partial(run, False), *args)


def solution(mesh):
    return jax.shard_map(
        body,
        mesh=mesh,
        in_specs=(
            P("blk", "head"),
            P(None, None, "head"),
            P(None, "head"),
            P(None, "blk", None, "head"),
            P(),
            P(),
            P(),
        ),
        out_specs=(P("blk", "head"), P(None, "blk", None, "head")),
        check_vma=False,
    )
```
